512 devices in a mesh: band: 32 (over x_hi, z), pw: 16 (over y, x_lo, core).
Axes of the slice: x: 4 (x_hi: 2, x_lo: 2; x = x_hi * 2 + x_lo), y: 4, z: 16, core: 2. Of those that a mesh axis runs over, the one named last changes fastest.
Arguments:
- orbitals: float32 [12288, 4096], P('pw', 'band'), may hold values from -0.0546875 to 0.0546875
- h_orbitals: float32 [12288, 4096], P('pw', 'band'), may hold values from -0.0546875 to 0.0546875
Outputs:
- margin_slots: float32 [4096, 2176], P(('band', 'pw'))
- hamilton_slots: float32 [4096, 2176], P(('band', 'pw'))
The draws below stay inside these ranges and needn't reach their ends.
All inputs are finite; a program needn't handle non-finite values.
Results may differ from the reference program's by a relative error of at most 0.0003.
Values sent between devices are 32-bit elements; how exact they have to be, the bound alone decides.
A program may use at most 64 MiB of HBM per device.

```python
import jax
import jax.numpy as jnp
from jax import lax

BAND_DEV = 128
NB = 4096
NPW = 12288
SLOTS = 17
N_BAND = 32


def steps_of(own_key, shape, pieces, low, largest):
    def one(dim, blocks):
        steps = jax.random.uniform(jax.random.fold_in(jax.random.fold_in(own_key, 6), dim), (blocks,), jnp.float32, low / len(pieces), largest / len(pieces))
        return jnp.repeat(jnp.exp(steps), shape[dim] // blocks).reshape((-1,) + (1,) * (len(shape) - dim - 1))

    level = one(*pieces[0])
    for cut in pieces[1:]:
        level = level * one(*cut)
    return level


def gaussian(rng, extent, width, most, pieces=(), kind=jnp.bfloat16):
    entries = width * jax.random.normal(rng, extent, jnp.float32)
    if pieces:
        entries = entries * steps_of(rng, extent, pieces, -0.22, 0.18)
    return jnp.clip(entries, -most, most).astype(kind)


def setup_inputs(seed: int = 0) -> dict:
    key_list = jax.random.split(jax.random.key(seed), 3)
    orbitals = gaussian(key_list[0], (NPW, NB), NPW ** -0.5, 0.0546875, ((0, 16), (1, 32)), jnp.float32)
    h_orbitals = gaussian(key_list[1], (NPW, NB), NPW ** -0.5, 0.0546875, ((0, 16), (1, 32)), jnp.float32)
    return {"orbitals": orbitals, "h_orbitals": h_orbitals}


def reference(orbitals, h_orbitals):
    doubled_psi = jnp.concatenate([orbitals, orbitals], axis=1)
    doubled_h = jnp.concatenate([h_orbitals, h_orbitals], axis=1)

    def one_block(block_index):
        first_col = (block_index * BAND_DEV).astype(jnp.int32)
        row_block = lax.dynamic_slice_in_dim(orbitals, first_col, BAND_DEV, 1)
        psi_cols = lax.dynamic_slice_in_dim(doubled_psi, first_col, SLOTS * BAND_DEV, 1)
        h_cols = lax.dynamic_slice_in_dim(doubled_h, first_col, SLOTS * BAND_DEV, 1)
        margin = jnp.dot(row_block.T, psi_cols, precision=lax.Precision.HIGHEST, preferred_element_type=jnp.float32)
        hamilton = jnp.dot(row_block.T, h_cols, precision=lax.Precision.HIGHEST, preferred_element_type=jnp.float32)
        return margin, hamilton

    margin_all, hamilton_all = lax.map(one_block, jnp.arange(N_BAND, dtype=jnp.int32))
    return (margin_all.reshape(NB, SLOTS * BAND_DEV), hamilton_all.reshape(NB, SLOTS * BAND_DEV))
```

```python
import functools

import jax
import jax.numpy as jnp
from jax import lax
from jax.experimental import pallas as pl
from jax.experimental.pallas import tpu as pltpu
from jax.sharding import PartitionSpec as P

MESH = pl.DeviceIdType.MESH
F32, BF16 = jnp.float32, jnp.bfloat16


def split(values):
    high = values.astype(BF16)
    return high, (values - high.astype(F32)).astype(BF16)


def dot(left, right):
    return jnp.dot(left, right, preferred_element_type=F32)


def kernel(
    bands, slabs, pieces, psi_ref, h_ref, margin_ref, hamilton_ref,
    block, high_w, low_w, total, core_in, core_sum, plane_in, result,
    ring_send, ring_recv, core_send, core_recv, plane_send, plane_recv, home_send, home_recv,
):
    half, groups = bands // 2, slabs // 2
    steps = half // 2
    width = psi_ref.shape[1]
    depth = psi_ref.shape[0] // pieces
    rows = width // slabs
    band, slab = lax.axis_index("band"), lax.axis_index("pw")
    core, group = lax.rem(slab, 2), lax.div(slab, 2)
    up = (lax.rem(band + 1, bands), slab)
    down = (lax.rem(band + bands - 1, bands), slab)
    across = (lax.rem(band + half, bands), slab)
    twin = (band, 2 * group + 1 - core)

    def plane_peer(distance):
        return (band, 2 * lax.rem(group + distance, groups) + core)

    barrier = pltpu.get_barrier_semaphore()
    partners = [up, down, across, twin] + [plane_peer(d) for d in range(1, groups)]
    for partner in partners:
        pl.semaphore_signal(barrier, inc=1, device_id=partner, device_id_type=MESH)

    for j in range(pieces):
        turned = psi_ref[pl.ds(j * depth, depth), :].T
        for g in range(groups):
            for c in range(2):
                block[0, j, pl.ds((c * groups + g) * rows, rows), :] = turned[(2 * g + c) * rows : (2 * g + c + 1) * rows, :]
    pl.semaphore_wait(barrier, len(partners))

    def ring(source, target, j, send, device):
        return pltpu.make_async_remote_copy(
            src_ref=block.at[source, j], dst_ref=block.at[target, j], send_sem=ring_send.at[send, j],
            recv_sem=ring_recv.at[target, j], device_id=device, device_id_type=MESH,
        )

    def go_up(k, j):
        return ring(k, k + 1, j, k, up)

    def go_down(k, j):
        return ring(k, k - 1, j, k, down)

    def go_across(j):
        return ring(0, half, j, steps, across)

    for j in range(pieces):
        go_up(0, j).start()
        go_across(j).start()

    for j in range(pieces):
        for ref, lanes in ((psi_ref, slice(0, width)), (h_ref, slice(width, 2 * width))):
            high, low = split(ref[pl.ds(j * depth, depth), :])
            high_w[j, :, lanes] = high
            low_w[j, :, lanes] = low

    def multiply(s, slots, j):
        highs, lows = zip(*[split(block[k, j]) for k in slots])
        n = len(slots)
        upper = dot(jnp.concatenate(highs + lows, axis=0), high_w[j])
        lower = dot(jnp.concatenate(highs, axis=0), low_w[j])
        for i in range(n):
            part = (
                upper[i * width : (i + 1) * width]
                + (upper[(n + i) * width : (n + i + 1) * width] + lower[i * width : (i + 1) * width])
            )
            if j == 0:
                total[s, i] = part
            else:
                total[s, i] += part

    def core_copy(s, n):
        theirs = pl.ds(pl.multiple_of((1 - core) * (width // 2), width // 2), width // 2)
        return pltpu.make_async_remote_copy(
            src_ref=total.at[s, pl.ds(0, n), theirs], dst_ref=core_in.at[s, pl.ds(0, n)],
            send_sem=core_send.at[s], recv_sem=core_recv.at[s], device_id=twin, device_id_type=MESH,
        )

    def plane_copy(s, n, distance):
        peer = lax.rem(group + distance, groups)
        theirs = pl.ds(pl.multiple_of(peer * rows, rows), rows)
        return pltpu.make_async_remote_copy(
            src_ref=core_sum.at[s, pl.ds(0, n), theirs], dst_ref=plane_in.at[s, distance - 1, pl.ds(0, n)],
            send_sem=plane_send.at[s], recv_sem=plane_recv.at[s],
            device_id=plane_peer(distance), device_id_type=MESH,
        )

    def plane_all(s, n):
        everything = plane_in.at[s, :, pl.ds(0, n)]
        return pltpu.make_async_remote_copy(
            src_ref=everything, dst_ref=everything, send_sem=plane_send.at[s], recv_sem=plane_recv.at[s],
            device_id=plane_peer(1), device_id_type=MESH,
        )

    def home_copy(s, i, k, which):
        out = (margin_ref, hamilton_ref)[which]
        there = pl.ds(pl.multiple_of(k * width, width), width)
        return pltpu.make_async_remote_copy(
            src_ref=result.at[s, i, :, pl.ds(which * width, width)], dst_ref=out.at[:, there],
            send_sem=home_send.at[k, which], recv_sem=home_recv.at[k, which],
            device_id=(lax.rem(band + bands - k, bands), slab), device_id_type=MESH,
        )

    def to_twin(s, n):
        core_copy(s, n).start()

    def to_plane(s, n):
        core_copy(s, n).wait_recv()
        mine = pl.ds(pl.multiple_of(core * (width // 2), width // 2), width // 2)
        for i in range(n):
            core_sum[s, i] = total[s, i, mine, :] + core_in[s, i]
        for d in range(1, groups):
            plane_copy(s, n, d).start()

    def summed(s, i):
        value = core_sum[s, i, pl.ds(pl.multiple_of(group * rows, rows), rows), :]
        for d in range(1, groups):
            value = value + plane_in[s, d - 1, i]
        return value

    def to_home(s):
        plane_all(s, 2).wait_recv()
        for i, k in enumerate((s, half + 1 - s)):
            result[s, i] = summed(s, i)
            for which in range(2):
                home_copy(s, i, k, which).start()

    for j in range(pieces):
        multiply(0, (0,), j)
    to_twin(0, 1)

    def step(s, _):
        other = half + 1 - s
        for j in range(pieces):
            go_up(s - 1, j).wait_recv()

            @pl.when(s < steps)
            def _():
                go_up(s, j).start()

            ring(0, other, j, 0, up).wait_recv()

            @pl.when(s < steps)
            def _():
                go_down(other, j).start()

            multiply(s, (s, other), j)
            if j == 0:
                @pl.when(s > 1)
                def _():
                    to_plane(s - 1, 2)
            if j == 1:
                @pl.when(s > 2)
                def _():
                    to_home(s - 2)
            if j == 2:
                @pl.when(s == 1)
                def _():
                    to_plane(0, 1)
        to_twin(s, 2)
        return 0

    lax.fori_loop(1, steps + 1, step, 0)
    to_plane(steps, 2)
    to_home(steps - 1)
    plane_all(0, 1).wait_recv()
    own = summed(0, 0)
    margin_ref[:, pl.ds(0, width)] = own[:, :width]
    hamilton_ref[:, pl.ds(0, width)] = own[:, width:]
    to_home(steps)

    def ring_sent(k, _):
        for j in range(pieces):
            ring(k, 0, j, k, up).wait_send()
        return 0

    lax.fori_loop(0, steps + 1, ring_sent, 0)
    lax.fori_loop(steps + 2, half + 1, ring_sent, 0)
    core_copy(0, 1).wait_send()
    plane_all(0, 1).wait_send()

    def sums_sent(s, _):
        core_copy(s, 2).wait_send()
        plane_all(s, 2).wait_send()
        return 0

    lax.fori_loop(1, steps + 1, sums_sent, 0)

    def home_done(k, _):
        for which in range(2):
            home_copy(0, 0, k, which).wait()
        return 0

    lax.fori_loop(1, half + 1, home_done, 0)


def solution(mesh):
    bands, slabs = mesh.shape["band"], mesh.shape["pw"]
    half, groups = bands // 2, slabs // 2
    steps = half // 2
    pieces = 3

    def shards(psi, h):
        depth, width = psi.shape
        rows = width // slabs
        out = jax.ShapeDtypeStruct((rows, (half + 1) * width), F32)
        vmem = pl.BlockSpec(memory_space=pltpu.VMEM)
        dma = pltpu.SemaphoreType.DMA
        return pl.pallas_call(
            functools.partial(kernel, bands, slabs, pieces),
            out_shape=(out, out),
            in_specs=[vmem, vmem],
            out_specs=(vmem, vmem),
            scratch_shapes=[
                pltpu.VMEM((half + 1, pieces, width, depth // pieces), F32),
                pltpu.VMEM((pieces, depth // pieces, 2 * width), BF16),
                pltpu.VMEM((pieces, depth // pieces, 2 * width), BF16),
                pltpu.VMEM((steps + 1, 2, width, 2 * width), F32),
                pltpu.VMEM((steps + 1, 2, width // 2, 2 * width), F32),
                pltpu.VMEM((steps + 1, 2, width // 2, 2 * width), F32),
                pltpu.VMEM((steps + 1, groups - 1, 2, rows, 2 * width), F32),
                pltpu.VMEM((steps + 1, 2, rows, 2 * width), F32),
                dma((half + 1, pieces)),
                dma((half + 1, pieces)),
                dma((steps + 1,)),
                dma((steps + 1,)),
                dma((steps + 1,)),
                dma((steps + 1,)),
                dma((half + 1, 2)),
                dma((half + 1, 2)),
            ],
            compiler_params=pltpu.CompilerParams(
                collective_id=0, has_side_effects=True, vmem_limit_bytes=40 << 20
            ),
            cost_estimate=pl.CostEstimate(
                flops=6 * (half + 1) * depth * width * 2 * width,
                bytes_accessed=4 * (2 * depth * width + 2 * rows * (half + 1) * width),
                transcendentals=0,
            ),
        )(psi, h)

    return jax.shard_map(
        shards,
        mesh=mesh,
        in_specs=(P("pw", "band"), P("pw", "band")),
        out_specs=(P(("band", "pw"), None), P(("band", "pw"), None)),
        check_vma=False,
    )
```

```python
import functools

import jax
import jax.numpy as jnp
from jax import lax
from jax.experimental import pallas as pl
from jax.experimental.pallas import tpu as pltpu
from jax.sharding import PartitionSpec as P

MESH = pl.DeviceIdType.MESH
F32, BF16 = jnp.float32, jnp.bfloat16


def split(values):
    high = values.astype(BF16)
    return high, (values - high.astype(F32)).astype(BF16)


def kernel(
    bands, slabs, psi_hbm, h_hbm, margin_ref, hamilton_ref,
    psi, h, turned_away, image, block, weight, total, core_in, core_sum, plane_in, result,
    load_sem, ring_send, ring_recv, across_send, across_recv, image_send, image_recv,
    core_send, core_recv, plane_send, plane_recv, home_send, home_recv,
):
    planes, groups = bands // 2, slabs // 2
    last = planes // 2
    depth, width = psi.shape[0] // 2, psi.shape[1]
    half = width // 2
    rows = width // slabs
    band, slab = lax.axis_index("band"), lax.axis_index("pw")
    side, plane = lax.div(band, planes), lax.rem(band, planes)
    group, core = lax.div(slab, 2), lax.rem(slab, 2)

    def at_plane(distance):
        return (side * planes + lax.rem(plane + distance + planes, planes), slab)

    def plane_peer(distance):
        there = lax.rem(side + distance // groups, 2)
        return (there * planes + plane, 2 * lax.rem(group + distance % groups, groups) + core)

    up, down, across = at_plane(1), at_plane(-1), plane_peer(groups)
    twin = (band, 2 * group + 1 - core)

    def load(i):
        return pltpu.make_async_copy((psi_hbm, h_hbm)[i], (psi, h)[i], load_sem.at[i])

    load(0).start()
    load(1).start()
    barrier = pltpu.get_barrier_semaphore()
    partners = [up, down, twin] + [plane_peer(d) for d in range(1, 2 * groups)]
    for partner in partners:
        pl.semaphore_signal(barrier, inc=1, device_id=partner, device_id_type=MESH)

    mine = pl.ds(pl.multiple_of(side * depth, depth), depth)
    theirs = pl.ds(pl.multiple_of((1 - side) * depth, depth), depth)

    def turn(part, ref, lead):
        turned = psi[part, :].T
        for c in range(2):
            for g in range(groups):
                place = (2 * g + c) * rows
                ref[lead + (c, pl.ds(g * rows, rows), slice(None))] = turned[place : place + rows, :]

    load(0).wait()
    turn(mine, block, (0, 0))
    turn(theirs, turned_away, ())
    load(1).wait()
    pl.semaphore_wait(barrier, len(partners))

    def ring(source, target, o, r, send, device):
        return pltpu.make_async_remote_copy(
            src_ref=block.at[source, o, r], dst_ref=block.at[target, o, r], send_sem=ring_send.at[send, o, r],
            recv_sem=ring_recv.at[target, o, r], device_id=device, device_id_type=MESH,
        )

    def go_up(s, o, r):
        return ring(s, s + 1, o, r, s, up)

    def go_down(s, o, r):
        source = 0 if isinstance(s, int) and s == 0 else last + s
        return ring(source, last + s + 1, o, r, last + s, down)

    def hand_across(r):
        return pltpu.make_async_remote_copy(
            src_ref=turned_away.at[r], dst_ref=block.at[0, 1, r], send_sem=across_send.at[r],
            recv_sem=across_recv.at[r], device_id=across, device_id_type=MESH,
        )

    def hand_image(i):
        return pltpu.make_async_remote_copy(
            src_ref=(psi, h)[i].at[theirs], dst_ref=image.at[i], send_sem=image_send.at[i],
            recv_sem=image_recv.at[i], device_id=across, device_id_type=MESH,
        )

    for r in range(2):
        go_up(0, 0, r).start()
        go_down(0, 0, r).start()
        hand_across(r).start()
    for i in range(2):
        hand_image(i).start()

    def weigh(o, values, lanes):
        high, low = split(values)
        weight[o, pl.ds(0, depth), lanes] = high
        weight[o, pl.ds(depth, depth), lanes] = low
        weight[o, pl.ds(2 * depth, depth), lanes] = high

    weigh(0, psi[mine, :], slice(0, width))
    weigh(0, h[mine, :], slice(width, 2 * width))
    for r in range(2):
        hand_across(r).wait_recv()
        go_up(0, 1, r).start()
        go_down(0, 1, r).start()

    def left(n, o):
        values = jnp.concatenate([block[n, o, 0], block[n, o, 1]], axis=0)
        high, low = split(values)
        return jnp.concatenate([high, high, low], axis=1)

    def multiply(s, sources):
        for o in range(2):
            ours = [lax.rem(o + turn_over, 2) for _, turn_over in sources]
            lefts = [left(n(w), w) for w, (n, _) in zip(ours, sources)]
            product = jnp.dot(jnp.concatenate(lefts, axis=0), weight[o], preferred_element_type=F32)
            for u, w in enumerate(ours):
                total[s, u, w] = product[u * width : (u + 1) * width]

    def multiply_pair(s):
        above = jnp.where(s == 0, 0, last + s)
        multiply(s, (
            (lambda o: s, jnp.where(plane < s, 1, 0)),
            (lambda o: above, jnp.where(plane + s < planes, 1, 0)),
        ))

    def multiply_last():
        multiply(last, ((lambda o: last * (1 + o), jnp.where(plane < last, 1, 0)),))

    def core_copy(s, n):
        return pltpu.make_async_remote_copy(
            src_ref=total.at[s, pl.ds(0, n), :, pl.ds(pl.multiple_of((1 - core) * half, half), half)],
            dst_ref=core_in.at[s, pl.ds(0, n)],
            send_sem=core_send.at[s], recv_sem=core_recv.at[s], device_id=twin, device_id_type=MESH,
        )

    def plane_copy(s, n, distance):
        there = lax.rem(group + distance % groups, groups)
        return pltpu.make_async_remote_copy(
            src_ref=core_sum.at[s, pl.ds(0, n), distance // groups, pl.ds(pl.multiple_of(there * rows, rows), rows)],
            dst_ref=plane_in.at[s, distance - 1, pl.ds(0, n)],
            send_sem=plane_send.at[s], recv_sem=plane_recv.at[s],
            device_id=plane_peer(distance), device_id_type=MESH,
        )

    def plane_all(s, n):
        everything = plane_in.at[s, :, pl.ds(0, n)]
        return pltpu.make_async_remote_copy(
            src_ref=everything, dst_ref=everything, send_sem=plane_send.at[s], recv_sem=plane_recv.at[s],
            device_id=across, device_id_type=MESH,
        )

    def home_copy(s, u, k, which, device):
        out = (margin_ref, hamilton_ref)[which]
        return pltpu.make_async_remote_copy(
            src_ref=result.at[s, u, :, pl.ds(which * width, width)],
            dst_ref=out.at[:, pl.ds(pl.multiple_of(k * width, width), width)],
            send_sem=home_send.at[k, which], recv_sem=home_recv.at[k, which], device_id=device, device_id_type=MESH,
        )

    def to_twin(s, n):
        core_copy(s, n).start()

    def to_plane(s, n):
        core_copy(s, n).wait_recv()
        ours = pl.ds(pl.multiple_of(core * half, half), half)
        for u in range(n):
            for o in range(2):
                core_sum[s, u, o] = total[s, u, o, ours, :] + core_in[s, u, o]
        for d in range(1, 2 * groups):
            plane_copy(s, n, d).start()

    def summed(s, u):
        value = core_sum[s, u, 0, pl.ds(pl.multiple_of(group * rows, rows), rows), :]
        for d in range(1, 2 * groups):
            value = value + plane_in[s, d - 1, u]
        return value

    def to_home(s, n):
        plane_all(s, n).wait_recv()
        for u in range(n):
            result[s, u] = summed(s, u)
            for which in range(2):
                home_copy(s, u, planes - s if u else s, which, at_plane(s if u else -s)).start()

    def stay_home():
        plane_all(0, 2).wait_recv()
        for u, k in ((0, 0), (1, planes)):
            value = summed(0, u)
            margin_ref[:, pl.ds(k * width, width)] = value[:, :width]
            hamilton_ref[:, pl.ds(k * width, width)] = value[:, width:]

    def step(s, _):
        for o in range(2):
            for r in range(2):
                go_up(s - 1, o, r).wait_recv()
                if o == 0:
                    go_up(s, o, r).start()
                else:
                    pl.when(s < last - 1)(lambda: go_up(s, o, r).start())
                ring(0, last + s, o, r, 0, down).wait_recv()
                if o == 1:
                    go_down(s, o, r).start()
                else:
                    pl.when(s < last - 1)(lambda: go_down(s, o, r).start())
                if (o, r) == (0, 0):
                    pl.when(s > 1)(lambda: to_plane(s - 2, 2))
                if (o, r) == (0, 1):
                    pl.when(s > 3)(lambda: to_home(s - 3, 2))

        @pl.when(s == 1)
        def _():
            for i in range(2):
                hand_image(i).wait_recv()
                weigh(1, image[i], slice(i * width, (i + 1) * width))

        multiply_pair(s - 1)
        to_twin(s - 1, 2)
        return 0

    lax.fori_loop(1, last, step, 0)
    multiply_pair(last - 1)
    to_twin(last - 1, 2)
    to_plane(last - 2, 2)
    to_home(last - 3, 2)
    for r in range(2):
        go_up(last - 1, 0, r).wait_recv()
        ring(0, 2 * last, 1, r, 0, down).wait_recv()
    multiply_last()
    to_twin(last, 1)
    to_plane(last - 1, 2)
    to_plane(last, 1)
    to_home(last - 2, 2)
    stay_home()
    to_home(last - 1, 2)
    to_home(last, 1)

    def ring_sent(s, _):
        for o in range(2):
            for r in range(2):
                ring(0, 1, o, r, s, up).wait_send()
        return 0

    lax.fori_loop(0, last - 1, ring_sent, 0)
    lax.fori_loop(last, 2 * last - 1, ring_sent, 0)
    for r in range(2):
        ring(0, 1, 0, r, last - 1, up).wait_send()
        ring(0, 1, 1, r, 2 * last - 1, up).wait_send()
        hand_across(r).wait_send()
        hand_image(r).wait_send()

    def sums_sent(s, _):
        core_copy(s, 2).wait_send()
        plane_all(s, 2).wait_send()
        return 0

    lax.fori_loop(0, last, sums_sent, 0)
    core_copy(last, 1).wait_send()
    plane_all(last, 1).wait_send()

    def home_done(k, _):
        for which in range(2):
            home_copy(0, 0, k, which, up).wait()
        return 0

    lax.fori_loop(1, planes, home_done, 0)


def solution(mesh):
    bands, slabs = mesh.shape["band"], mesh.shape["pw"]
    planes, groups = bands // 2, slabs // 2
    last = planes // 2

    def shards(psi, h):
        depth, width = psi.shape[0] // 2, psi.shape[1]
        half, rows = width // 2, width // slabs
        out = jax.ShapeDtypeStruct((rows, (planes + 1) * width), F32)
        vmem, anywhere = pl.BlockSpec(memory_space=pltpu.VMEM), pl.BlockSpec(memory_space=pl.ANY)
        dma = pltpu.SemaphoreType.DMA
        return pl.pallas_call(
            functools.partial(kernel, bands, slabs),
            out_shape=(out, out),
            in_specs=[anywhere, anywhere],
            out_specs=(vmem, vmem),
            scratch_shapes=[
                pltpu.VMEM(psi.shape, F32),
                pltpu.VMEM(h.shape, F32),
                pltpu.VMEM((2, half, depth), F32),
                pltpu.VMEM((2, depth, width), F32),
                pltpu.VMEM((planes + 1, 2, 2, half, depth), F32),
                pltpu.VMEM((2, 3 * depth, 2 * width), BF16),
                pltpu.VMEM((last + 1, 2, 2, width, 2 * width), F32),
                pltpu.VMEM((last + 1, 2, 2, half, 2 * width), F32),
                pltpu.VMEM((last + 1, 2, 2, half, 2 * width), F32),
                pltpu.VMEM((last + 1, 2 * groups - 1, 2, rows, 2 * width), F32),
                pltpu.VMEM((last + 1, 2, rows, 2 * width), F32),
                dma((2,)),
                dma((planes, 2, 2)),
                dma((planes + 1, 2, 2)),
                dma((2,)),
                dma((2,)),
                dma((2,)),
                dma((2,)),
                dma((last + 1,)),
                dma((last + 1,)),
                dma((last + 1,)),
                dma((last + 1,)),
                dma((planes, 2)),
                dma((planes, 2)),
            ],
            compiler_params=pltpu.CompilerParams(
                collective_id=0, has_side_effects=True, vmem_limit_bytes=48 << 20
            ),
            cost_estimate=pl.CostEstimate(
                flops=6 * (planes + 1) * 2 * depth * width * 2 * width,
                bytes_accessed=4 * (4 * depth * width + 2 * rows * (planes + 1) * width),
                transcendentals=0,
            ),
        )(psi, h)

    return jax.shard_map(
        shards,
        mesh=mesh,
        in_specs=(P("pw", "band"), P("pw", "band")),
        out_specs=(P(("band", "pw"), None), P(("band", "pw"), None)),
        check_vma=False,
    )
```

```python
import functools

import jax
import jax.numpy as jnp
from jax import lax
from jax.experimental import pallas as pl
from jax.experimental.pallas import tpu as pltpu
from jax.sharding import PartitionSpec as P

MESH = pl.DeviceIdType.MESH
F32, BF16 = jnp.float32, jnp.bfloat16


def split(values):
    high = values.astype(BF16)
    return high, (values - high.astype(F32)).astype(BF16)


def kernel(
    bands, slabs, psi_hbm, h_hbm, margin_ref, hamilton_ref,
    psi, h, turned_away, image, block, weight, total, core_in, core_sum, plane_in, result,
    load_sem, ring_send, ring_recv, across_send, across_recv, image_send, image_recv,
    core_send, core_recv, plane_send, plane_recv, home_send, home_recv,
):
    planes, groups = bands // 2, slabs // 2
    pairs = planes // 2
    parts = block.shape[3]
    depth, width = psi.shape[0] // 2, psi.shape[1]
    half = width // 2
    rows = width // slabs
    band, slab = lax.axis_index("band"), lax.axis_index("pw")
    side, plane = lax.div(band, planes), lax.rem(band, planes)
    group, core = lax.div(slab, 2), lax.rem(slab, 2)

    def at_plane(distance):
        return (side * planes + lax.rem(plane + distance + planes, planes), slab)

    def plane_peer(distance):
        there = lax.rem(side + distance // groups, 2)
        return (there * planes + plane, 2 * lax.rem(group + distance % groups, groups) + core)

    up, down, across = at_plane(1), at_plane(-1), plane_peer(groups)
    twin = (band, 2 * group + 1 - core)

    def load(i):
        return pltpu.make_async_copy((psi_hbm, h_hbm)[i], (psi, h)[i], load_sem.at[i])

    load(0).start()
    load(1).start()
    barrier = pltpu.get_barrier_semaphore()
    partners = [up, down, twin] + [plane_peer(d) for d in range(1, 2 * groups)]
    for partner in partners:
        pl.semaphore_signal(barrier, inc=1, device_id=partner, device_id_type=MESH)

    mine = pl.ds(pl.multiple_of(side * depth, depth), depth)
    theirs = pl.ds(pl.multiple_of((1 - side) * depth, depth), depth)

    def turn(part, ref, lead):
        turned = psi[part, :].T
        for c in range(2):
            for g in range(groups):
                place = (2 * g + c) * rows
                piece, row = divmod(g * rows, half // parts)
                ref[lead(c, piece) + (pl.ds(row, rows), slice(None))] = turned[place : place + rows, :]

    load(0).wait()
    turn(mine, block, lambda c, piece: (0, c, 0, piece))
    turn(theirs, turned_away, lambda c, piece: (c, piece))
    load(1).wait()
    pl.semaphore_wait(barrier, len(partners))

    def ring(s, r, o, j):
        return pltpu.make_async_remote_copy(
            src_ref=block.at[s, r, o, j], dst_ref=block.at[s + 1, r, o, j], send_sem=ring_send.at[s, r, o, j],
            recv_sem=ring_recv.at[s + 1, r, o, j], device_id=(up, down)[r], device_id_type=MESH,
        )

    def hand_across(r, j):
        return pltpu.make_async_remote_copy(
            src_ref=turned_away.at[r, j], dst_ref=block.at[0, r, 1, j], send_sem=across_send.at[r, j],
            recv_sem=across_recv.at[r, j], device_id=across, device_id_type=MESH,
        )

    def hand_image(i):
        return pltpu.make_async_remote_copy(
            src_ref=(psi, h)[i].at[theirs], dst_ref=image.at[i], send_sem=image_send.at[i],
            recv_sem=image_recv.at[i], device_id=across, device_id_type=MESH,
        )

    for j in range(parts):
        for r in range(2):
            ring(0, r, 0, j).start()
            hand_across(r, j).start()
    for i in range(2):
        hand_image(i).start()

    def weigh(o, values, lanes):
        high, low = split(values)
        weight[o, pl.ds(0, depth), lanes] = high
        weight[o, pl.ds(depth, depth), lanes] = low
        weight[o, pl.ds(2 * depth, depth), lanes] = high

    weigh(0, psi[mine, :], slice(0, width))
    weigh(0, h[mine, :], slice(width, 2 * width))

    def pass_on(s, o, j):
        for r in range(2):
            ring(s - 1, r, o, j).wait_recv()
            ring(s, r, o, j).start()

    def left(s, r, o):
        high, low = split(block[s, r, o].reshape(half, depth))
        return jnp.concatenate([high, high, low], axis=1)

    def multiply(pair, sources):
        for o in range(2):
            places = [(u, r, s, lax.rem(o + crossed[r], 2)) for u, (s, crossed) in enumerate(sources) for r in range(2)]
            lefts = jnp.concatenate([left(s, r, w) for _, r, s, w in places], axis=0)
            product = jnp.dot(lefts, weight[o], preferred_element_type=F32)
            for i, (u, r, _, w) in enumerate(places):
                total[pair, u, r, w] = product[i * half : (i + 1) * half]

    def crossings(s):
        return jnp.where(plane < s, 1, 0), jnp.where(plane + s < planes, 1, 0)

    def core_copy(pair, n):
        return pltpu.make_async_remote_copy(
            src_ref=total.at[pair, pl.ds(0, n), 1 - core], dst_ref=core_in.at[pair, pl.ds(0, n)],
            send_sem=core_send.at[pair], recv_sem=core_recv.at[pair], device_id=twin, device_id_type=MESH,
        )

    def plane_copy(pair, n, distance):
        there = lax.rem(group + distance % groups, groups)
        return pltpu.make_async_remote_copy(
            src_ref=core_sum.at[pair, pl.ds(0, n), distance // groups, pl.ds(pl.multiple_of(there * rows, rows), rows)],
            dst_ref=plane_in.at[pair, distance - 1, pl.ds(0, n)],
            send_sem=plane_send.at[pair], recv_sem=plane_recv.at[pair],
            device_id=plane_peer(distance), device_id_type=MESH,
        )

    def plane_all(pair, n):
        everything = plane_in.at[pair, :, pl.ds(0, n)]
        return pltpu.make_async_remote_copy(
            src_ref=everything, dst_ref=everything, send_sem=plane_send.at[pair], recv_sem=plane_recv.at[pair],
            device_id=across, device_id_type=MESH,
        )

    def home_copy(pair, u, s, which):
        out = (margin_ref, hamilton_ref)[which]
        k = s + core * (planes - 2 * s)
        return pltpu.make_async_remote_copy(
            src_ref=result.at[pair, u, :, pl.ds(which * width, width)],
            dst_ref=out.at[:, pl.ds(pl.multiple_of(k * width, width), width)],
            send_sem=home_send.at[k, which], recv_sem=home_recv.at[k, which],
            device_id=at_plane((2 * core - 1) * s), device_id_type=MESH,
        )

    def to_twin(pair, n):
        core_copy(pair, n).start()

    def sum_cores(pair, n):
        core_copy(pair, n).wait_recv()
        for u in range(n):
            for o in range(2):
                core_sum[pair, u, o] = total[pair, u, core, o] + core_in[pair, u, o]

    def to_plane(pair, n, distances):
        for d in distances:
            plane_copy(pair, n, d).start()

    peers = range(1, 2 * groups)

    def summed(pair, u):
        value = core_sum[pair, u, 0, pl.ds(pl.multiple_of(group * rows, rows), rows), :]
        for d in peers:
            value = value + plane_in[pair, d - 1, u]
        return value

    def sum_plane(pair, n):
        plane_all(pair, n).wait_recv()
        for u in range(n):
            result[pair, u] = summed(pair, u)

    def to_home(pair, n):
        for u in range(n):
            for which in range(2):
                home_copy(pair, u, 2 * pair - 1 + u, which).start()

    def stay_home():
        plane_all(0, 2).wait_recv()
        for u, k in ((0, 0), (1, planes)):
            value = summed(0, u)
            margin_ref[:, pl.ds(k * width, width)] = value[:, :width]
            hamilton_ref[:, pl.ds(k * width, width)] = value[:, width:]

    def multiply_pair(pair):
        multiply(pair, [(s, crossings(s)) for s in (2 * pair - 1, 2 * pair)])

    for j in range(parts):
        pass_on(1, 0, j)
        for r in range(2):
            hand_across(r, j).wait_recv()
            ring(0, r, 1, j).start()
    for s, o in ((1, 1), (2, 0), (2, 1)):
        for j in range(parts):
            pass_on(s, o, j)

    def two_steps(pair, _):
        def work(event):
            if event == 0:
                @pl.when(pair == 3)
                def _():
                    sum_cores(0, 2)
                    to_plane(0, 2, peers)
            if event == 3:
                @pl.when(pair == 2)
                def _():
                    for i in range(2):
                        hand_image(i).wait_recv()
                        weigh(1, image[i], slice(i * width, (i + 1) * width))
            if event == 4:
                multiply_pair(pair - 1)
                to_twin(pair - 1, 2)
            if event == 5:
                @pl.when(pair == 2)
                def _():
                    multiply(0, [(0, (0, 0)), (0, (1, 1))])
                    to_twin(0, 2)

                @pl.when(pair > 2)
                def _():
                    sum_plane(pair - 2, 2)
            if event == 6:
                sum_cores(pair - 1, 2)
                to_plane(pair - 1, 2, peers[: len(peers) // 2])
            if event == 7:
                to_plane(pair - 1, 2, peers[len(peers) // 2 :])

        events = 4 * parts
        for event in range(events):
            step, o, j = event // (2 * parts), event // parts % 2, event % parts
            pass_on(2 * pair - 1 + step, o, j)
            for e in range(event * 8 // events, (event + 1) * 8 // events):
                work(e)
        return 0

    lax.fori_loop(2, pairs, two_steps, 0)
    multiply_pair(pairs - 1)
    to_twin(pairs - 1, 2)

    def go_home(pair, _):
        to_home(pair, 2)
        return 0

    lax.fori_loop(1, pairs - 2, go_home, 0)
    sum_cores(pairs - 1, 2)
    to_plane(pairs - 1, 2, peers)
    for o in range(2):
        for j in range(parts):
            for r in range(2):
                ring(planes - 2, r, o, j).wait_recv()
    multiply(pairs, [(planes - 1, crossings(planes - 1))])
    to_twin(pairs, 1)
    sum_plane(pairs - 2, 2)
    to_home(pairs - 2, 2)
    sum_cores(pairs, 1)
    to_plane(pairs, 1, peers)

    def ring_sent(s, _):
        for r in range(2):
            for o in range(2):
                for j in range(parts):
                    ring(s, r, o, j).wait_send()
        return 0

    lax.fori_loop(0, planes - 1, ring_sent, 0)
    for r in range(2):
        hand_image(r).wait_send()
        for j in range(parts):
            hand_across(r, j).wait_send()

    def sums_sent(pair, _):
        core_copy(pair, 2).wait_send()
        plane_all(pair, 2).wait_send()
        return 0

    lax.fori_loop(0, pairs, sums_sent, 0)
    stay_home()
    sum_plane(pairs - 1, 2)
    to_home(pairs - 1, 2)
    sum_plane(pairs, 1)
    to_home(pairs, 1)
    core_copy(pairs, 1).wait_send()
    plane_all(pairs, 1).wait_send()

    def home_done(s, _):
        for which in range(2):
            home_copy(0, 0, s, which).wait()
        return 0

    lax.fori_loop(1, planes, home_done, 0)


def solution(mesh):
    bands, slabs = mesh.shape["band"], mesh.shape["pw"]
    planes, groups = bands // 2, slabs // 2
    pairs, parts = planes // 2, 2

    def shards(psi, h):
        depth, width = psi.shape[0] // 2, psi.shape[1]
        half, rows = width // 2, width // slabs
        out = jax.ShapeDtypeStruct((rows, (planes + 1) * width), F32)
        vmem, anywhere = pl.BlockSpec(memory_space=pltpu.VMEM), pl.BlockSpec(memory_space=pl.ANY)
        dma = pltpu.SemaphoreType.DMA
        return pl.pallas_call(
            functools.partial(kernel, bands, slabs),
            out_shape=(out, out),
            in_specs=[anywhere, anywhere],
            out_specs=(vmem, vmem),
            scratch_shapes=[
                pltpu.VMEM(psi.shape, F32),
                pltpu.VMEM(h.shape, F32),
                pltpu.VMEM((2, parts, half // parts, depth), F32),
                pltpu.VMEM((2, depth, width), F32),
                pltpu.VMEM((planes, 2, 2, parts, half // parts, depth), F32),
                pltpu.VMEM((2, 3 * depth, 2 * width), BF16),
                pltpu.VMEM((pairs + 1, 2, 2, 2, half, 2 * width), F32),
                pltpu.VMEM((pairs + 1, 2, 2, half, 2 * width), F32),
                pltpu.VMEM((pairs + 1, 2, 2, half, 2 * width), F32),
                pltpu.VMEM((pairs + 1, 2 * groups - 1, 2, rows, 2 * width), F32),
                pltpu.VMEM((pairs + 1, 2, rows, 2 * width), F32),
                dma((2,)),
                dma((planes - 1, 2, 2, parts)),
                dma((planes, 2, 2, parts)),
                dma((2, parts)),
                dma((2, parts)),
                dma((2,)),
                dma((2,)),
                dma((pairs + 1,)),
                dma((pairs + 1,)),
                dma((pairs + 1,)),
                dma((pairs + 1,)),
                dma((planes, 2)),
                dma((planes, 2)),
            ],
            compiler_params=pltpu.CompilerParams(
                collective_id=0, has_side_effects=True, vmem_limit_bytes=54900 << 10
            ),
            cost_estimate=pl.CostEstimate(
                flops=6 * (planes + 1) * 2 * depth * width * 2 * width,
                bytes_accessed=4 * (4 * depth * width + 2 * rows * (planes + 1) * width),
                transcendentals=0,
            ),
        )(psi, h)

    return jax.shard_map(
        shards,
        mesh=mesh,
        in_specs=(P("pw", "band"), P("pw", "band")),
        out_specs=(P(("band", "pw"), None), P(("band", "pw"), None)),
        check_vma=False,
    )
```

```python
import functools

import jax
import jax.numpy as jnp
from jax import lax
from jax.experimental import pallas as pl
from jax.experimental.pallas import tpu as pltpu
from jax.sharding import PartitionSpec as P

MESH = pl.DeviceIdType.MESH
F32, BF16 = jnp.float32, jnp.bfloat16


def split(values):
    high = values.astype(BF16)
    return high, (values - high.astype(F32)).astype(BF16)


def kernel(
    bands, slabs, psi_hbm, h_hbm, margin_ref, hamilton_ref,
    psi, h, turned_away, image, block, weight, total, core_in, core_sum, plane_in, result, home_in, direct_in,
    load_sem, ring_send, ring_recv, across_send, across_recv, image_send, image_recv,
    core_send, core_recv, plane_send, plane_recv, home_send, home_recv, direct_send, direct_recv,
):
    planes, groups = bands // 2, slabs // 2
    pairs = planes // 2 - 1
    end = planes - 1
    parts = block.shape[3]
    depth, width = psi.shape[0] // 2, psi.shape[1]
    half = width // 2
    rows = width // slabs
    band, slab = lax.axis_index("band"), lax.axis_index("pw")
    side, plane = lax.div(band, planes), lax.rem(band, planes)
    group, core = lax.div(slab, 2), lax.rem(slab, 2)

    def at_plane(distance):
        return (side * planes + lax.rem(plane + distance + planes, planes), slab)

    def plane_peer(distance):
        there = lax.rem(side + distance // groups, 2)
        return (there * planes + plane, 2 * lax.rem(group + distance % groups, groups) + core)

    up, down, across = at_plane(1), at_plane(-1), plane_peer(groups)
    twin = (band, 2 * group + 1 - core)

    def load(i):
        return pltpu.make_async_copy((psi_hbm, h_hbm)[i], (psi, h)[i], load_sem.at[i])

    load(0).start()
    load(1).start()
    barrier = pltpu.get_barrier_semaphore()
    partners = [up, down, twin] + [plane_peer(d) for d in range(1, 2 * groups)]
    for partner in partners:
        pl.semaphore_signal(barrier, inc=1, device_id=partner, device_id_type=MESH)

    mine = pl.ds(pl.multiple_of(side * depth, depth), depth)
    theirs = pl.ds(pl.multiple_of((1 - side) * depth, depth), depth)

    def turn(part, ref, lead):
        turned = psi[part, :].T
        for c in range(2):
            for g in range(groups):
                place = (2 * g + c) * rows
                piece, row = divmod(g * rows, half // parts)
                ref[lead(c, piece) + (pl.ds(row, rows), slice(None))] = turned[place : place + rows, :]

    load(0).wait()
    turn(mine, block, lambda c, piece: (0, c, 0, piece))
    turn(theirs, turned_away, lambda c, piece: (c, piece))
    load(1).wait()
    pl.semaphore_wait(barrier, len(partners))

    def ring(s, r, o, j):
        return pltpu.make_async_remote_copy(
            src_ref=block.at[s, r, o, j], dst_ref=block.at[s + 1, r, o, j], send_sem=ring_send.at[s, r, o, j],
            recv_sem=ring_recv.at[s + 1, r, o, j], device_id=(up, down)[r], device_id_type=MESH,
        )

    def hand_across(r, j):
        return pltpu.make_async_remote_copy(
            src_ref=turned_away.at[r, j], dst_ref=block.at[0, r, 1, j], send_sem=across_send.at[r, j],
            recv_sem=across_recv.at[r, j], device_id=across, device_id_type=MESH,
        )

    def hand_image(i):
        return pltpu.make_async_remote_copy(
            src_ref=(psi, h)[i].at[theirs], dst_ref=image.at[i], send_sem=image_send.at[i],
            recv_sem=image_recv.at[i], device_id=across, device_id_type=MESH,
        )

    for j in range(parts):
        for r in range(2):
            ring(0, r, 0, j).start()
            hand_across(r, j).start()

    def weigh(o, values, lanes):
        high, low = split(values)
        weight[o, pl.ds(0, depth), lanes] = high
        weight[o, pl.ds(depth, depth), lanes] = low
        weight[o, pl.ds(2 * depth, depth), lanes] = high

    weigh(0, psi[mine, :], slice(0, width))
    weigh(0, h[mine, :], slice(width, 2 * width))

    def pass_on(s, o, j):
        for r in range(2):
            ring(s - 1, r, o, j).wait_recv()
            ring(s, r, o, j).start()
        if not (isinstance(s, int) and s == 1):
            for r in range(2):
                ring(s - 1, r, o, j).wait_send()

    def left(s, r, o):
        high, low = split(block[s, r, o].reshape(half, depth))
        return jnp.concatenate([high, high, low], axis=1)

    def multiply(pair, sources):
        for o in range(2):
            places = [(u, r, s, lax.rem(o + crossed[r], 2)) for u, (s, crossed) in enumerate(sources) for r in range(2)]
            lefts = jnp.concatenate([left(s, r, w) for _, r, s, w in places], axis=0)
            product = jnp.dot(lefts, weight[o], preferred_element_type=F32)
            for i, (u, r, _, w) in enumerate(places):
                total[pair, u, r, w] = product[i * half : (i + 1) * half]

    def crossings(s):
        return jnp.where(plane < s, 1, 0), jnp.where(plane + s < planes, 1, 0)

    def core_copy(pair, n):
        return pltpu.make_async_remote_copy(
            src_ref=total.at[pair, pl.ds(0, n), 1 - core], dst_ref=core_in.at[pair, pl.ds(0, n)],
            send_sem=core_send.at[pair], recv_sem=core_recv.at[pair], device_id=twin, device_id_type=MESH,
        )

    def plane_copy(pair, n, distance):
        there = lax.rem(group + distance % groups, groups)
        return pltpu.make_async_remote_copy(
            src_ref=core_sum.at[pair, pl.ds(0, n), distance // groups, pl.ds(pl.multiple_of(there * rows, rows), rows)],
            dst_ref=plane_in.at[pair, distance - 1, pl.ds(0, n)],
            send_sem=plane_send.at[pair], recv_sem=plane_recv.at[pair],
            device_id=plane_peer(distance), device_id_type=MESH,
        )

    def plane_all(pair, n):
        everything = plane_in.at[pair, :, pl.ds(0, n)]
        return pltpu.make_async_remote_copy(
            src_ref=everything, dst_ref=everything, send_sem=plane_send.at[pair], recv_sem=plane_recv.at[pair],
            device_id=across, device_id_type=MESH,
        )

    def first_step(group_index):
        return group_index + (end - pairs - 2) if isinstance(group_index, int) and group_index >= pairs else 2 * group_index - 1

    def home_copy(pair, u, s):
        k = s + core * (planes - 2 * s)
        return pltpu.make_async_remote_copy(
            src_ref=result.at[pair, u], dst_ref=home_in.at[k], send_sem=home_send.at[0], recv_sem=home_recv.at[0],
            device_id=at_plane((2 * core - 1) * s), device_id_type=MESH,
        )

    def home_all():
        everything = home_in.at[pl.ds(1 + core, end - 1)]
        return pltpu.make_async_remote_copy(
            src_ref=everything, dst_ref=everything, send_sem=home_send.at[0], recv_sem=home_recv.at[0],
            device_id=up, device_id_type=MESH,
        )

    def direct_copy(distance):
        there = lax.rem(group + distance % groups, groups)
        side_there = lax.rem(side + distance // groups, 2)
        plane_there = lax.rem(plane + (2 * core - 1) * end + planes, planes)
        return pltpu.make_async_remote_copy(
            src_ref=core_sum.at[pairs + 2, 0, distance // groups, pl.ds(pl.multiple_of(there * rows, rows), rows)],
            dst_ref=direct_in.at[distance], send_sem=direct_send.at[0], recv_sem=direct_recv.at[0],
            device_id=(side_there * planes + plane_there, 2 * there + core), device_id_type=MESH,
        )

    def direct_all():
        return pltpu.make_async_remote_copy(
            src_ref=direct_in, dst_ref=direct_in, send_sem=direct_send.at[0], recv_sem=direct_recv.at[0],
            device_id=up, device_id_type=MESH,
        )

    def half_copy(o):
        return pltpu.make_async_remote_copy(
            src_ref=total.at[pairs + 2, 0, 1 - core, o], dst_ref=core_in.at[pairs + 2, 0, o],
            send_sem=core_send.at[pairs + 2 + o], recv_sem=core_recv.at[pairs + 2 + o], device_id=twin, device_id_type=MESH,
        )

    def to_twin(pair, n):
        core_copy(pair, n).start()

    def sum_cores(pair, n):
        core_copy(pair, n).wait()
        for u in range(n):
            for o in range(2):
                core_sum[pair, u, o] = total[pair, u, core, o] + core_in[pair, u, o]

    def to_plane(pair, n, distances):
        for d in distances:
            plane_copy(pair, n, d).start()

    peers = range(1, 2 * groups)

    def summed(pair, u):
        value = core_sum[pair, u, 0, pl.ds(pl.multiple_of(group * rows, rows), rows), :]
        for d in peers:
            value = value + plane_in[pair, d - 1, u]
        return value

    def sum_plane(pair, n):
        plane_all(pair, n).wait()
        for u in range(n):
            result[pair, u] = summed(pair, u)

    def to_home(pair, n):
        for u in range(n):
            home_copy(pair, u, first_step(pair) + u).start()

    def deliver(k, value):
        margin_ref[:, pl.ds(k * width, width)] = value[:, :width]
        hamilton_ref[:, pl.ds(k * width, width)] = value[:, width:]

    def stay_home():
        plane_all(0, 2).wait()
        deliver(0, summed(0, 0))
        deliver(planes, summed(0, 1))

    def multiply_pair(pair):
        multiply(pair, [(s, crossings(s)) for s in (2 * pair - 1, 2 * pair)])

    def multiply_single(pair):
        s = first_step(pair)
        multiply(pair, [(s, crossings(s))])

    for j in range(parts):
        pass_on(1, 0, j)
        for r in range(2):
            hand_across(r, j).wait_recv()
            ring(0, r, 1, j).start()
    for i in range(2):
        hand_image(i).start()
    for s, o in ((1, 1), (2, 0), (2, 1)):
        for j in range(parts):
            pass_on(s, o, j)

    front, back = peers[: len(peers) // 2], peers[len(peers) // 2 :]

    def two_steps(pair, work):
        events = 4 * parts
        for event in range(events):
            step, o, j = event // (2 * parts), event // parts % 2, event % parts
            pass_on(2 * pair - 1 + step, o, j)
            for e in range(event * 8 // events, (event + 1) * 8 // events):
                work(e)

    def turn_of(pair, _):
        def work(event):
            if event == 0:
                @pl.when(pair == 3)
                def _():
                    sum_cores(0, 2)
                    to_plane(0, 2, peers)
            if event == 3:
                @pl.when(pair == 2)
                def _():
                    for i in range(2):
                        hand_image(i).wait_recv()
                        weigh(1, image[i], slice(i * width, (i + 1) * width))
            if event == 4:
                multiply_pair(pair - 1)
                to_twin(pair - 1, 2)
            if event == 5:
                @pl.when(pair == 2)
                def _():
                    multiply(0, [(0, (0, 0)), (0, (1, 1))])
                    to_twin(0, 2)

                @pl.when(pair > 2)
                def _():
                    sum_plane(pair - 2, 2)

                @pl.when((pair > 2) & (pair < pairs - 2))
                def _():
                    to_home(pair - 2, 2)
                @pl.when(pair == 4)
                def _():
                    stay_home()
            if event == 6:
                sum_cores(pair - 1, 2)
                to_plane(pair - 1, 2, front)
            if event == 7:
                to_plane(pair - 1, 2, back)

        two_steps(pair, work)
        return 0

    lax.fori_loop(2, pairs, turn_of, 0)

    def last_turn(event):
        if event == 0:
            multiply_pair(pairs - 1)
            to_twin(pairs - 1, 2)
        if event == 1:
            sum_plane(pairs - 2, 2)
        if event == 2:
            sum_cores(pairs - 1, 2)
            to_plane(pairs - 1, 2, front)
        if event == 3:
            to_plane(pairs - 1, 2, back)
        if event == 4:
            multiply_single(pairs)
            to_twin(pairs, 1)
        if event == 6:
            sum_cores(pairs, 1)
            to_plane(pairs, 1, front)
        if event == 7:
            to_plane(pairs, 1, back)

    two_steps(pairs, last_turn)
    multiply_single(pairs + 1)
    to_twin(pairs + 1, 1)

    def go_home(pair, _):
        to_home(pair, 2)
        return 0

    lax.fori_loop(pairs - 4, pairs - 1, go_home, 0)
    sum_cores(pairs + 1, 1)
    to_plane(pairs + 1, 1, peers)

    crossed = crossings(end)
    for o in range(2):
        for j in range(parts):
            for r in range(2):
                ring(end - 1, r, o, j).wait_recv()
        for r in range(2):
            product = jnp.dot(left(end, r, o), weight[lax.rem(o + crossed[r], 2)], preferred_element_type=F32)
            total[pairs + 2, 0, r, o] = product
        half_copy(o).start()
        if o == 0:
            sum_plane(pairs - 1, 2)
            to_home(pairs - 1, 2)
            half_copy(o).wait_recv()
            core_sum[pairs + 2, 0, o] = total[pairs + 2, 0, core, o] + core_in[pairs + 2, 0, o]
            for d in range(groups):
                direct_copy(d).start()
    sum_plane(pairs, 1)
    to_home(pairs, 1)
    half_copy(1).wait_recv()
    core_sum[pairs + 2, 0, 1] = total[pairs + 2, 0, core, 1] + core_in[pairs + 2, 0, 1]
    for d in range(groups, 2 * groups):
        direct_copy(d).start()
    sum_plane(pairs + 1, 1)
    to_home(pairs + 1, 1)

    for r in range(2):
        hand_image(r).wait_send()
        for j in range(parts):
            hand_across(r, j).wait_send()
            for o in range(2):
                ring(0, r, o, j).wait_send()
                ring(end - 1, r, o, j).wait_send()
    for o in range(2):
        half_copy(o).wait_send()
    home_all().wait()
    for k in range(2, end):
        deliver(k, home_in[k])
    for c in range(2):
        @pl.when(core == c)
        def _():
            deliver(1 + c * (end - 1), home_in[1 + c * (end - 1)])
    direct_all().wait()
    value = direct_in[0]
    for d in range(1, 2 * groups):
        value = value + direct_in[d]
    for c in range(2):
        @pl.when(core == c)
        def _():
            deliver(end - c * (end - 1), value)


def solution(mesh):
    bands, slabs = mesh.shape["band"], mesh.shape["pw"]
    planes, groups = bands // 2, slabs // 2
    pairs, parts = planes // 2 - 1, 2

    def shards(psi, h):
        depth, width = psi.shape[0] // 2, psi.shape[1]
        half, rows = width // 2, width // slabs
        out = jax.ShapeDtypeStruct((rows, (planes + 1) * width), F32)
        vmem, anywhere = pl.BlockSpec(memory_space=pltpu.VMEM), pl.BlockSpec(memory_space=pl.ANY)
        dma = pltpu.SemaphoreType.DMA
        return pl.pallas_call(
            functools.partial(kernel, bands, slabs),
            out_shape=(out, out),
            in_specs=[anywhere, anywhere],
            out_specs=(vmem, vmem),
            scratch_shapes=[
                pltpu.VMEM(psi.shape, F32),
                pltpu.VMEM(h.shape, F32),
                pltpu.VMEM((2, parts, half // parts, depth), F32),
                pltpu.VMEM((2, depth, width), F32),
                pltpu.VMEM((planes, 2, 2, parts, half // parts, depth), F32),
                pltpu.VMEM((2, 3 * depth, 2 * width), BF16),
                pltpu.VMEM((pairs + 3, 2, 2, 2, half, 2 * width), F32),
                pltpu.VMEM((pairs + 3, 2, 2, half, 2 * width), F32),
                pltpu.VMEM((pairs + 3, 2, 2, half, 2 * width), F32),
                pltpu.VMEM((pairs + 3, 2 * groups - 1, 2, rows, 2 * width), F32),
                pltpu.VMEM((pairs + 3, 2, rows, 2 * width), F32),
                pltpu.VMEM((planes, rows, 2 * width), F32),
                pltpu.VMEM((2 * groups, rows, 2 * width), F32),
                dma((2,)),
                dma((planes - 1, 2, 2, parts)),
                dma((planes, 2, 2, parts)),
                dma((2, parts)),
                dma((2, parts)),
                dma((2,)),
                dma((2,)),
                dma((pairs + 4,)),
                dma((pairs + 4,)),
                dma((pairs + 4,)),
                dma((pairs + 4,)),
                dma((1,)),
                dma((1,)),
                dma((1,)),
                dma((1,)),
            ],
            compiler_params=pltpu.CompilerParams(
                collective_id=0, has_side_effects=True, vmem_limit_bytes=54900 << 10
            ),
            cost_estimate=pl.CostEstimate(
                flops=6 * (planes + 1) * 2 * depth * width * 2 * width,
                bytes_accessed=4 * (4 * depth * width + 2 * rows * (planes + 1) * width),
                transcendentals=0,
            ),
        )(psi, h)

    return jax.shard_map(
        shards,
        mesh=mesh,
        in_specs=(P("pw", "band"), P("pw", "band")),
        out_specs=(P(("band", "pw"), None), P(("band", "pw"), None)),
        check_vma=False,
    )
```

```python
import functools

import jax
import jax.numpy as jnp
from jax import lax
from jax.experimental import pallas as pl
from jax.experimental.pallas import tpu as pltpu
from jax.sharding import PartitionSpec as P

MESH = pl.DeviceIdType.MESH
F32, BF16 = jnp.float32, jnp.bfloat16


def split(values):
    high = values.astype(BF16)
    return high, (values - high.astype(F32)).astype(BF16)


def kernel(
    bands, slabs, psi_hbm, h_hbm, margin_ref, hamilton_ref,
    psi, h, turned_away, image, block, weight, total, core_in, core_sum, plane_in, result, home_in, direct_in,
    load_sem, ring_send, ring_recv, across_send, across_recv, image_send, image_recv,
    core_send, core_recv, plane_send, plane_recv, home_send, home_recv, direct_send, direct_recv,
):
    planes, groups = bands // 2, slabs // 2
    pairs = planes // 2 - 1
    end = planes - 1
    parts = block.shape[3]
    depth, width = psi.shape[0] // 2, psi.shape[1]
    half = width // 2
    rows = width // slabs
    band, slab = lax.axis_index("band"), lax.axis_index("pw")
    side, plane = lax.div(band, planes), lax.rem(band, planes)
    group, core = lax.div(slab, 2), lax.rem(slab, 2)

    def at_plane(distance):
        return (side * planes + lax.rem(plane + distance + planes, planes), slab)

    def plane_peer(distance):
        there = lax.rem(side + distance // groups, 2)
        return (there * planes + plane, 2 * lax.rem(group + distance % groups, groups) + core)

    up, down, across = at_plane(1), at_plane(-1), plane_peer(groups)
    twin = (band, 2 * group + 1 - core)

    def load(i):
        return pltpu.make_async_copy((psi_hbm, h_hbm)[i], (psi, h)[i], load_sem.at[i])

    load(0).start()
    load(1).start()
    barrier = pltpu.get_barrier_semaphore()
    partners = [up, down, twin] + [plane_peer(d) for d in range(1, 2 * groups)]
    for partner in partners:
        pl.semaphore_signal(barrier, inc=1, device_id=partner, device_id_type=MESH)

    mine = pl.ds(pl.multiple_of(side * depth, depth), depth)
    theirs = pl.ds(pl.multiple_of((1 - side) * depth, depth), depth)

    def turn(part, ref, lead):
        turned = psi[part, :].T
        for c in range(2):
            for g in range(groups):
                place = (2 * g + c) * rows
                piece, row = divmod(g * rows, half // parts)
                ref[lead(c, piece) + (pl.ds(row, rows), slice(None))] = turned[place : place + rows, :]

    load(0).wait()
    turn(mine, block, lambda c, piece: (0, c, 0, piece))
    turn(theirs, turned_away, lambda c, piece: (c, piece))
    load(1).wait()
    pl.semaphore_wait(barrier, len(partners))

    def ring(s, r, o, j):
        return pltpu.make_async_remote_copy(
            src_ref=block.at[s, r, o, j], dst_ref=block.at[s + 1, r, o, j], send_sem=ring_send.at[s, r, o, j],
            recv_sem=ring_recv.at[s + 1, r, o, j], device_id=(up, down)[r], device_id_type=MESH,
        )

    def hand_across(r, j):
        return pltpu.make_async_remote_copy(
            src_ref=turned_away.at[r, j], dst_ref=block.at[0, r, 1, j], send_sem=across_send.at[r, j],
            recv_sem=across_recv.at[r, j], device_id=across, device_id_type=MESH,
        )

    def hand_image(i):
        return pltpu.make_async_remote_copy(
            src_ref=(psi, h)[i].at[theirs], dst_ref=image.at[i], send_sem=image_send.at[i],
            recv_sem=image_recv.at[i], device_id=across, device_id_type=MESH,
        )

    for j in range(parts):
        for r in range(2):
            ring(0, r, 0, j).start()
            hand_across(r, j).start()

    def weigh(o, values, lanes):
        high, low = split(values)
        weight[o, pl.ds(0, depth), lanes] = high
        weight[o, pl.ds(depth, depth), lanes] = low
        weight[o, pl.ds(2 * depth, depth), lanes] = high

    weigh(0, psi[mine, :], slice(0, width))
    weigh(0, h[mine, :], slice(width, 2 * width))

    def pass_on(s, o, j):
        for r in range(2):
            ring(s - 1, r, o, j).wait_recv()
            ring(s, r, o, j).start()
        if not (isinstance(s, int) and s == 1):
            for r in range(2):
                ring(s - 1, r, o, j).wait_send()

    def left(s, r, o):
        high, low = split(block[s, r, o].reshape(half, depth))
        return jnp.concatenate([high, high, low], axis=1)

    def multiply(pair, sources):
        for o in range(2):
            places = [(u, r, s, lax.rem(o + crossed[r], 2)) for u, (s, crossed) in enumerate(sources) for r in range(2)]
            lefts = jnp.concatenate([left(s, r, w) for _, r, s, w in places], axis=0)
            product = jnp.dot(lefts, weight[o], preferred_element_type=F32)
            for i, (u, r, _, w) in enumerate(places):
                total[pair, u, r, w] = product[i * half : (i + 1) * half]

    def crossings(s):
        return jnp.where(plane < s, 1, 0), jnp.where(plane + s < planes, 1, 0)

    def core_copy(pair, n):
        return pltpu.make_async_remote_copy(
            src_ref=total.at[pair, pl.ds(0, n), 1 - core], dst_ref=core_in.at[pair, pl.ds(0, n)],
            send_sem=core_send.at[pair], recv_sem=core_recv.at[pair], device_id=twin, device_id_type=MESH,
        )

    def plane_copy(pair, n, distance):
        there = lax.rem(group + distance % groups, groups)
        return pltpu.make_async_remote_copy(
            src_ref=core_sum.at[pair, pl.ds(0, n), distance // groups, pl.ds(pl.multiple_of(there * rows, rows), rows)],
            dst_ref=plane_in.at[pair, distance - 1, pl.ds(0, n)],
            send_sem=plane_send.at[pair], recv_sem=plane_recv.at[pair],
            device_id=plane_peer(distance), device_id_type=MESH,
        )

    def plane_all(pair, n):
        everything = plane_in.at[pair, :, pl.ds(0, n)]
        return pltpu.make_async_remote_copy(
            src_ref=everything, dst_ref=everything, send_sem=plane_send.at[pair], recv_sem=plane_recv.at[pair],
            device_id=across, device_id_type=MESH,
        )

    def first_step(group_index):
        return group_index + (end - pairs - 2) if isinstance(group_index, int) and group_index >= pairs else 2 * group_index - 1

    def home_copy(pair, u, s):
        k = s + core * (planes - 2 * s)
        return pltpu.make_async_remote_copy(
            src_ref=result.at[pair, u], dst_ref=home_in.at[k], send_sem=home_send.at[0], recv_sem=home_recv.at[0],
            device_id=at_plane((2 * core - 1) * s), device_id_type=MESH,
        )

    def home_all():
        everything = home_in.at[pl.ds(1 + core, end - 1)]
        return pltpu.make_async_remote_copy(
            src_ref=everything, dst_ref=everything, send_sem=home_send.at[0], recv_sem=home_recv.at[0],
            device_id=up, device_id_type=MESH,
        )

    def direct_copy(distance):
        there = lax.rem(group + distance % groups, groups)
        side_there = lax.rem(side + distance // groups, 2)
        plane_there = lax.rem(plane + (2 * core - 1) * end + planes, planes)
        return pltpu.make_async_remote_copy(
            src_ref=core_sum.at[pairs + 2, 0, distance // groups, pl.ds(pl.multiple_of(there * rows, rows), rows)],
            dst_ref=direct_in.at[distance], send_sem=direct_send.at[0], recv_sem=direct_recv.at[0],
            device_id=(side_there * planes + plane_there, 2 * there + core), device_id_type=MESH,
        )

    def direct_all():
        return pltpu.make_async_remote_copy(
            src_ref=direct_in, dst_ref=direct_in, send_sem=direct_send.at[0], recv_sem=direct_recv.at[0],
            device_id=up, device_id_type=MESH,
        )

    def half_copy(o):
        return pltpu.make_async_remote_copy(
            src_ref=total.at[pairs + 2, 0, 1 - core, o], dst_ref=core_in.at[pairs + 2, 0, o],
            send_sem=core_send.at[pairs + 2 + o], recv_sem=core_recv.at[pairs + 2 + o], device_id=twin, device_id_type=MESH,
        )

    def to_twin(pair, n):
        core_copy(pair, n).start()

    def sum_cores(pair, n):
        core_copy(pair, n).wait()
        for u in range(n):
            for o in range(2):
                core_sum[pair, u, o] = total[pair, u, core, o] + core_in[pair, u, o]

    def to_plane(pair, n, distances):
        for d in distances:
            plane_copy(pair, n, d).start()

    around = sorted(range(groups), key=lambda d: -min(d, groups - d))
    peers = sorted(range(1, 2 * groups), key=lambda d: -min(d % groups, -d % groups) - d // groups * (groups // 2))

    def summed(pair, u):
        value = core_sum[pair, u, 0, pl.ds(pl.multiple_of(group * rows, rows), rows), :]
        for d in peers:
            value = value + plane_in[pair, d - 1, u]
        return value

    def sum_plane(pair, n):
        plane_all(pair, n).wait()
        for u in range(n):
            result[pair, u] = summed(pair, u)

    def to_home(pair, n):
        for u in range(n):
            home_copy(pair, u, first_step(pair) + u).start()

    def deliver(k, value):
        margin_ref[:, pl.ds(k * width, width)] = value[:, :width]
        hamilton_ref[:, pl.ds(k * width, width)] = value[:, width:]

    def stay_home():
        plane_all(0, 2).wait()
        deliver(0, summed(0, 0))
        deliver(planes, summed(0, 1))

    def multiply_pair(pair):
        multiply(pair, [(s, crossings(s)) for s in (2 * pair - 1, 2 * pair)])

    def multiply_single(pair):
        s = first_step(pair)
        multiply(pair, [(s, crossings(s))])

    for j in range(parts):
        pass_on(1, 0, j)
        for r in range(2):
            hand_across(r, j).wait_recv()
            ring(0, r, 1, j).start()
    for i in range(2):
        hand_image(i).start()
    for s, o in ((1, 1), (2, 0), (2, 1)):
        for j in range(parts):
            pass_on(s, o, j)

    front, back = peers[: len(peers) // 2], peers[len(peers) // 2 :]

    def two_steps(pair, work):
        events = 4 * parts
        for event in range(events):
            step, o, j = event // (2 * parts), event // parts % 2, event % parts
            pass_on(2 * pair - 1 + step, o, j)
            for e in range(event * 8 // events, (event + 1) * 8 // events):
                work(e)

    def turn_of(pair, _):
        def work(event):
            if event == 0:
                @pl.when(pair == 3)
                def _():
                    sum_cores(0, 2)
                    to_plane(0, 2, peers)
            if event == 3:
                @pl.when(pair == 2)
                def _():
                    for i in range(2):
                        hand_image(i).wait_recv()
                        weigh(1, image[i], slice(i * width, (i + 1) * width))
            if event == 4:
                multiply_pair(pair - 1)
                to_twin(pair - 1, 2)
            if event == 5:
                @pl.when(pair == 2)
                def _():
                    multiply(0, [(0, (0, 0)), (0, (1, 1))])
                    to_twin(0, 2)

                @pl.when(pair > 2)
                def _():
                    sum_plane(pair - 2, 2)

                @pl.when((pair > 2) & (pair < pairs - 2))
                def _():
                    to_home(pair - 2, 2)
                @pl.when(pair == 4)
                def _():
                    stay_home()
            if event == 6:
                sum_cores(pair - 1, 2)
                to_plane(pair - 1, 2, front)
            if event == 7:
                to_plane(pair - 1, 2, back)

        two_steps(pair, work)
        return 0

    lax.fori_loop(2, pairs, turn_of, 0)

    def last_turn(event):
        if event == 0:
            multiply_pair(pairs - 1)
            to_twin(pairs - 1, 2)
        if event == 1:
            sum_plane(pairs - 2, 2)
        if event == 2:
            sum_cores(pairs - 1, 2)
            to_plane(pairs - 1, 2, front)
        if event == 3:
            to_plane(pairs - 1, 2, back)
        if event == 4:
            multiply_single(pairs)
            to_twin(pairs, 1)
        if event == 6:
            sum_cores(pairs, 1)
            to_plane(pairs, 1, front)
        if event == 7:
            to_plane(pairs, 1, back)

    two_steps(pairs, last_turn)
    multiply_single(pairs + 1)
    to_twin(pairs + 1, 1)

    def go_home(pair, _):
        to_home(pair, 2)
        return 0

    lax.fori_loop(pairs - 4, pairs - 1, go_home, 0)
    sum_cores(pairs + 1, 1)
    to_plane(pairs + 1, 1, peers)

    crossed = crossings(end)
    for o in range(2):
        for j in range(parts):
            for r in range(2):
                ring(end - 1, r, o, j).wait_recv()
        for r in range(2):
            product = jnp.dot(left(end, r, o), weight[lax.rem(o + crossed[r], 2)], preferred_element_type=F32)
            total[pairs + 2, 0, r, o] = product
        half_copy(o).start()
        if o == 0:
            sum_plane(pairs - 1, 2)
            to_home(pairs - 1, 2)
            half_copy(o).wait_recv()
            core_sum[pairs + 2, 0, o] = total[pairs + 2, 0, core, o] + core_in[pairs + 2, 0, o]
            for d in around:
                direct_copy(d).start()
    sum_plane(pairs, 1)
    to_home(pairs, 1)
    half_copy(1).wait_recv()
    core_sum[pairs + 2, 0, 1] = total[pairs + 2, 0, core, 1] + core_in[pairs + 2, 0, 1]
    for d in around:
        direct_copy(groups + d).start()
    sum_plane(pairs + 1, 1)
    to_home(pairs + 1, 1)

    for r in range(2):
        hand_image(r).wait_send()
        for j in range(parts):
            hand_across(r, j).wait_send()
            for o in range(2):
                ring(0, r, o, j).wait_send()
                ring(end - 1, r, o, j).wait_send()
    for o in range(2):
        half_copy(o).wait_send()
    home_all().wait()
    for k in range(2, end):
        deliver(k, home_in[k])
    for c in range(2):
        @pl.when(core == c)
        def _():
            deliver(1 + c * (end - 1), home_in[1 + c * (end - 1)])
    direct_all().wait()
    value = direct_in[0]
    for d in range(1, 2 * groups):
        value = value + direct_in[d]
    for c in range(2):
        @pl.when(core == c)
        def _():
            deliver(end - c * (end - 1), value)


def solution(mesh):
    bands, slabs = mesh.shape["band"], mesh.shape["pw"]
    planes, groups = bands // 2, slabs // 2
    pairs, parts = planes // 2 - 1, 2

    def shards(psi, h):
        depth, width = psi.shape[0] // 2, psi.shape[1]
        half, rows = width // 2, width // slabs
        out = jax.ShapeDtypeStruct((rows, (planes + 1) * width), F32)
        vmem, anywhere = pl.BlockSpec(memory_space=pltpu.VMEM), pl.BlockSpec(memory_space=pl.ANY)
        dma = pltpu.SemaphoreType.DMA
        return pl.pallas_call(
            functools.partial(kernel, bands, slabs),
            out_shape=(out, out),
            in_specs=[anywhere, anywhere],
            out_specs=(vmem, vmem),
            scratch_shapes=[
                pltpu.VMEM(psi.shape, F32),
                pltpu.VMEM(h.shape, F32),
                pltpu.VMEM((2, parts, half // parts, depth), F32),
                pltpu.VMEM((2, depth, width), F32),
                pltpu.VMEM((planes, 2, 2, parts, half // parts, depth), F32),
                pltpu.VMEM((2, 3 * depth, 2 * width), BF16),
                pltpu.VMEM((pairs + 3, 2, 2, 2, half, 2 * width), F32),
                pltpu.VMEM((pairs + 3, 2, 2, half, 2 * width), F32),
                pltpu.VMEM((pairs + 3, 2, 2, half, 2 * width), F32),
                pltpu.VMEM((pairs + 3, 2 * groups - 1, 2, rows, 2 * width), F32),
                pltpu.VMEM((pairs + 3, 2, rows, 2 * width), F32),
                pltpu.VMEM((planes, rows, 2 * width), F32),
                pltpu.VMEM((2 * groups, rows, 2 * width), F32),
                dma((2,)),
                dma((planes - 1, 2, 2, parts)),
                dma((planes, 2, 2, parts)),
                dma((2, parts)),
                dma((2, parts)),
                dma((2,)),
                dma((2,)),
                dma((pairs + 4,)),
                dma((pairs + 4,)),
                dma((pairs + 4,)),
                dma((pairs + 4,)),
                dma((1,)),
                dma((1,)),
                dma((1,)),
                dma((1,)),
            ],
            compiler_params=pltpu.CompilerParams(
                collective_id=0, has_side_effects=True, vmem_limit_bytes=54900 << 10
            ),
            cost_estimate=pl.CostEstimate(
                flops=6 * (planes + 1) * 2 * depth * width * 2 * width,
                bytes_accessed=4 * (4 * depth * width + 2 * rows * (planes + 1) * width),
                transcendentals=0,
            ),
        )(psi, h)

    return jax.shard_map(
        shards,
        mesh=mesh,
        in_specs=(P("pw", "band"), P("pw", "band")),
        out_specs=(P(("band", "pw"), None), P(("band", "pw"), None)),
        check_vma=False,
    )
```

```python
import functools

import jax
import jax.numpy as jnp
from jax import lax
from jax.experimental import pallas as pl
from jax.experimental.pallas import tpu as pltpu
from jax.sharding import PartitionSpec as P

MESH = pl.DeviceIdType.MESH
F32, BF16 = jnp.float32, jnp.bfloat16


def split(values):
    high = values.astype(BF16)
    return high, (values - high.astype(F32)).astype(BF16)


def kernel(
    bands, slabs, psi_hbm, h_hbm, margin_ref, hamilton_ref,
    psi, h, turned_away, image, block, weight, total, core_in, core_sum, plane_in, result, home_in, direct_in,
    load_sem, ring_send, ring_recv, across_send, across_recv, image_send, image_recv,
    core_send, core_recv, plane_send, plane_recv, home_send, home_recv, direct_send, direct_recv,
):
    planes, groups = bands // 2, slabs // 2
    pairs = planes // 2 - 1
    end = planes - 1
    parts = block.shape[3]
    depth, width = psi.shape[0] // 2, psi.shape[1]
    half = width // 2
    rows = width // slabs
    band, slab = lax.axis_index("band"), lax.axis_index("pw")
    side, plane = lax.div(band, planes), lax.rem(band, planes)
    group, core = lax.div(slab, 2), lax.rem(slab, 2)

    def at_plane(distance):
        return (side * planes + lax.rem(plane + distance + planes, planes), slab)

    def plane_peer(distance):
        there = lax.rem(side + distance // groups, 2)
        return (there * planes + plane, 2 * lax.rem(group + distance % groups, groups) + core)

    up, down, across = at_plane(1), at_plane(-1), plane_peer(groups)
    twin = (band, 2 * group + 1 - core)

    def load(i):
        return pltpu.make_async_copy((psi_hbm, h_hbm)[i], (psi, h)[i], load_sem.at[i])

    load(0).start()
    load(1).start()
    barrier = pltpu.get_barrier_semaphore()
    partners = [up, down, twin] + [plane_peer(d) for d in range(1, 2 * groups)]
    for partner in partners:
        pl.semaphore_signal(barrier, inc=1, device_id=partner, device_id_type=MESH)

    mine = pl.ds(pl.multiple_of(side * depth, depth), depth)
    theirs = pl.ds(pl.multiple_of((1 - side) * depth, depth), depth)

    def turn(part, ref, lead):
        turned = psi[part, :].T
        for c in range(2):
            for g in range(groups):
                place = (2 * g + c) * rows
                piece, row = divmod(g * rows, half // parts)
                ref[lead(c, piece) + (pl.ds(row, rows), slice(None))] = turned[place : place + rows, :]

    load(0).wait()
    turn(mine, block, lambda c, piece: (0, c, 0, piece))
    turn(theirs, turned_away, lambda c, piece: (c, piece))
    load(1).wait()
    pl.semaphore_wait(barrier, len(partners))

    def ring(s, r, o, j):
        return pltpu.make_async_remote_copy(
            src_ref=block.at[s, r, o, j], dst_ref=block.at[s + 1, r, o, j], send_sem=ring_send.at[s, r, o, j],
            recv_sem=ring_recv.at[s + 1, r, o, j], device_id=(up, down)[r], device_id_type=MESH,
        )

    def hand_across(r, j):
        return pltpu.make_async_remote_copy(
            src_ref=turned_away.at[r, j], dst_ref=block.at[0, r, 1, j], send_sem=across_send.at[r, j],
            recv_sem=across_recv.at[r, j], device_id=across, device_id_type=MESH,
        )

    def hand_image(i):
        return pltpu.make_async_remote_copy(
            src_ref=(psi, h)[i].at[theirs], dst_ref=image.at[i], send_sem=image_send.at[i],
            recv_sem=image_recv.at[i], device_id=across, device_id_type=MESH,
        )

    for j in range(parts):
        for r in range(2):
            ring(0, r, 0, j).start()
            hand_across(r, j).start()

    def weigh(o, values, lanes):
        high, low = split(values)
        weight[o, pl.ds(0, depth), lanes] = high
        weight[o, pl.ds(depth, depth), lanes] = low
        weight[o, pl.ds(2 * depth, depth), lanes] = high

    weigh(0, psi[mine, :], slice(0, width))
    weigh(0, h[mine, :], slice(width, 2 * width))

    def pass_on(s, o, j):
        for r in range(2):
            ring(s - 1, r, o, j).wait_recv()
            ring(s, r, o, j).start()
        if not (isinstance(s, int) and s == 1):
            for r in range(2):
                ring(s - 1, r, o, j).wait_send()

    def left(s, r, o):
        high, low = split(block[s, r, o].reshape(half, depth))
        return jnp.concatenate([high, high, low], axis=1)

    def multiply(pair, sources):
        for o in range(2):
            places = [(u, r, s, lax.rem(o + crossed[r], 2)) for u, (s, crossed) in enumerate(sources) for r in range(2)]
            lefts = jnp.concatenate([left(s, r, w) for _, r, s, w in places], axis=0)
            product = jnp.dot(lefts, weight[o], preferred_element_type=F32)
            for i, (u, r, _, w) in enumerate(places):
                total[pair, u, r, w] = product[i * half : (i + 1) * half]

    def crossings(s):
        return jnp.where(plane < s, 1, 0), jnp.where(plane + s < planes, 1, 0)

    def core_copy(pair, n):
        return pltpu.make_async_remote_copy(
            src_ref=total.at[pair, pl.ds(0, n), 1 - core], dst_ref=core_in.at[pair, pl.ds(0, n)],
            send_sem=core_send.at[pair], recv_sem=core_recv.at[pair], device_id=twin, device_id_type=MESH,
        )

    def plane_copy(pair, n, distance):
        there = lax.rem(group + distance % groups, groups)
        return pltpu.make_async_remote_copy(
            src_ref=core_sum.at[pair, pl.ds(0, n), distance // groups, pl.ds(pl.multiple_of(there * rows, rows), rows)],
            dst_ref=plane_in.at[pair, distance - 1, pl.ds(0, n)],
            send_sem=plane_send.at[pair], recv_sem=plane_recv.at[pair],
            device_id=plane_peer(distance), device_id_type=MESH,
        )

    def plane_all(pair, n):
        everything = plane_in.at[pair, :, pl.ds(0, n)]
        return pltpu.make_async_remote_copy(
            src_ref=everything, dst_ref=everything, send_sem=plane_send.at[pair], recv_sem=plane_recv.at[pair],
            device_id=across, device_id_type=MESH,
        )

    def first_step(group_index):
        return group_index + (end - pairs - 2) if isinstance(group_index, int) and group_index >= pairs else 2 * group_index - 1

    def home_copy(pair, u, s):
        k = s + core * (planes - 2 * s)
        return pltpu.make_async_remote_copy(
            src_ref=result.at[pair, u], dst_ref=home_in.at[k], send_sem=home_send.at[0], recv_sem=home_recv.at[0],
            device_id=at_plane((2 * core - 1) * s), device_id_type=MESH,
        )

    def home_all():
        everything = home_in.at[pl.ds(1 + core, end - 1)]
        return pltpu.make_async_remote_copy(
            src_ref=everything, dst_ref=everything, send_sem=home_send.at[0], recv_sem=home_recv.at[0],
            device_id=up, device_id_type=MESH,
        )

    def direct_copy(distance):
        there = lax.rem(group + distance % groups, groups)
        side_there = lax.rem(side + distance // groups, 2)
        plane_there = lax.rem(plane + (2 * core - 1) * end + planes, planes)
        return pltpu.make_async_remote_copy(
            src_ref=core_sum.at[pairs + 2, 0, distance // groups, pl.ds(pl.multiple_of(there * rows, rows), rows)],
            dst_ref=direct_in.at[distance], send_sem=direct_send.at[0], recv_sem=direct_recv.at[0],
            device_id=(side_there * planes + plane_there, 2 * there + core), device_id_type=MESH,
        )

    def direct_all():
        return pltpu.make_async_remote_copy(
            src_ref=direct_in, dst_ref=direct_in, send_sem=direct_send.at[0], recv_sem=direct_recv.at[0],
            device_id=up, device_id_type=MESH,
        )

    def half_copy(o):
        return pltpu.make_async_remote_copy(
            src_ref=total.at[pairs + 2, 0, 1 - core, o], dst_ref=core_in.at[pairs + 2, 0, o],
            send_sem=core_send.at[pairs + 2 + o], recv_sem=core_recv.at[pairs + 2 + o], device_id=twin, device_id_type=MESH,
        )

    def to_twin(pair, n):
        core_copy(pair, n).start()

    def sum_cores(pair, n):
        core_copy(pair, n).wait()
        for u in range(n):
            for o in range(2):
                core_sum[pair, u, o] = total[pair, u, core, o] + core_in[pair, u, o]

    def to_plane(pair, n, distances):
        for d in distances:
            plane_copy(pair, n, d).start()

    around = sorted(range(groups), key=lambda d: -min(d, groups - d))
    peers = sorted(
        range(1, 2 * groups),
        key=lambda d: -min(d % groups, -d % groups) - 2 * (1 if d % 2 else d // groups * 2),
    )

    def summed(pair, u):
        value = core_sum[pair, u, 0, pl.ds(pl.multiple_of(group * rows, rows), rows), :]
        for d in peers:
            value = value + plane_in[pair, d - 1, u]
        return value

    def sum_plane(pair, n):
        plane_all(pair, n).wait()
        for u in range(n):
            result[pair, u] = summed(pair, u)

    def to_home(pair, n):
        for u in range(n):
            home_copy(pair, u, first_step(pair) + u).start()

    def deliver(k, value):
        margin_ref[:, pl.ds(k * width, width)] = value[:, :width]
        hamilton_ref[:, pl.ds(k * width, width)] = value[:, width:]

    def stay_home():
        plane_all(0, 2).wait()
        deliver(0, summed(0, 0))
        deliver(planes, summed(0, 1))

    def multiply_pair(pair):
        multiply(pair, [(s, crossings(s)) for s in (2 * pair - 1, 2 * pair)])

    def multiply_single(pair):
        s = first_step(pair)
        multiply(pair, [(s, crossings(s))])

    for j in range(parts):
        pass_on(1, 0, j)
        for r in range(2):
            hand_across(r, j).wait_recv()
            ring(0, r, 1, j).start()
    for i in range(2):
        hand_image(i).start()
    for s, o in ((1, 1), (2, 0), (2, 1)):
        for j in range(parts):
            pass_on(s, o, j)

    front, back = peers[: len(peers) // 2], peers[len(peers) // 2 :]

    def two_steps(pair, work):
        events = 4 * parts
        for event in range(events):
            step, o, j = event // (2 * parts), event // parts % 2, event % parts
            pass_on(2 * pair - 1 + step, o, j)
            for e in range(event * 8 // events, (event + 1) * 8 // events):
                work(e)

    def turn_of(pair, _):
        def work(event):
            if event == 0:
                @pl.when(pair == 3)
                def _():
                    sum_cores(0, 2)
                    to_plane(0, 2, peers)
            if event == 3:
                @pl.when(pair == 2)
                def _():
                    for i in range(2):
                        hand_image(i).wait_recv()
                        weigh(1, image[i], slice(i * width, (i + 1) * width))
            if event == 4:
                multiply_pair(pair - 1)
                to_twin(pair - 1, 2)
            if event == 5:
                @pl.when(pair == 2)
                def _():
                    multiply(0, [(0, (0, 0)), (0, (1, 1))])
                    to_twin(0, 2)

                @pl.when(pair > 2)
                def _():
                    sum_plane(pair - 2, 2)

                @pl.when((pair > 2) & (pair < pairs - 2))
                def _():
                    to_home(pair - 2, 2)
                @pl.when(pair == 4)
                def _():
                    stay_home()
            if event == 6:
                sum_cores(pair - 1, 2)
                to_plane(pair - 1, 2, front)
            if event == 7:
                to_plane(pair - 1, 2, back)

        two_steps(pair, work)
        return 0

    lax.fori_loop(2, pairs, turn_of, 0)

    def last_turn(event):
        if event == 0:
            multiply_pair(pairs - 1)
            to_twin(pairs - 1, 2)
        if event == 1:
            sum_plane(pairs - 2, 2)
        if event == 2:
            sum_cores(pairs - 1, 2)
            to_plane(pairs - 1, 2, front)
        if event == 3:
            to_plane(pairs - 1, 2, back)
        if event == 4:
            multiply_single(pairs)
            to_twin(pairs, 1)
        if event == 6:
            sum_cores(pairs, 1)
            to_plane(pairs, 1, front)
        if event == 7:
            to_plane(pairs, 1, back)

    two_steps(pairs, last_turn)
    multiply_single(pairs + 1)
    to_twin(pairs + 1, 1)

    def go_home(pair, _):
        to_home(pair, 2)
        return 0

    lax.fori_loop(pairs - 4, pairs - 1, go_home, 0)
    sum_cores(pairs + 1, 1)
    to_plane(pairs + 1, 1, peers)

    crossed = crossings(end)
    for o in range(2):
        for j in range(parts):
            for r in range(2):
                ring(end - 1, r, o, j).wait_recv()
        for r in range(2):
            product = jnp.dot(left(end, r, o), weight[lax.rem(o + crossed[r], 2)], preferred_element_type=F32)
            total[pairs + 2, 0, r, o] = product
        half_copy(o).start()
        if o == 0:
            sum_plane(pairs - 1, 2)
            to_home(pairs - 1, 2)
            half_copy(o).wait_recv()
            core_sum[pairs + 2, 0, o] = total[pairs + 2, 0, core, o] + core_in[pairs + 2, 0, o]
            for d in around:
                direct_copy(d).start()
    sum_plane(pairs, 1)
    to_home(pairs, 1)
    half_copy(1).wait_recv()
    core_sum[pairs + 2, 0, 1] = total[pairs + 2, 0, core, 1] + core_in[pairs + 2, 0, 1]
    for d in around:
        direct_copy(groups + d).start()
    sum_plane(pairs + 1, 1)
    to_home(pairs + 1, 1)

    for r in range(2):
        hand_image(r).wait_send()
        for j in range(parts):
            hand_across(r, j).wait_send()
            for o in range(2):
                ring(0, r, o, j).wait_send()
                ring(end - 1, r, o, j).wait_send()
    for o in range(2):
        half_copy(o).wait_send()
    home_all().wait()
    for k in range(2, end):
        deliver(k, home_in[k])
    for c in range(2):
        @pl.when(core == c)
        def _():
            deliver(1 + c * (end - 1), home_in[1 + c * (end - 1)])
    direct_all().wait()
    value = direct_in[0]
    for d in range(1, 2 * groups):
        value = value + direct_in[d]
    for c in range(2):
        @pl.when(core == c)
        def _():
            deliver(end - c * (end - 1), value)


def solution(mesh):
    bands, slabs = mesh.shape["band"], mesh.shape["pw"]
    planes, groups = bands // 2, slabs // 2
    pairs, parts = planes // 2 - 1, 2

    def shards(psi, h):
        depth, width = psi.shape[0] // 2, psi.shape[1]
        half, rows = width // 2, width // slabs
        out = jax.ShapeDtypeStruct((rows, (planes + 1) * width), F32)
        vmem, anywhere = pl.BlockSpec(memory_space=pltpu.VMEM), pl.BlockSpec(memory_space=pl.ANY)
        dma = pltpu.SemaphoreType.DMA
        return pl.pallas_call(
            functools.partial(kernel, bands, slabs),
            out_shape=(out, out),
            in_specs=[anywhere, anywhere],
            out_specs=(vmem, vmem),
            scratch_shapes=[
                pltpu.VMEM(psi.shape, F32),
                pltpu.VMEM(h.shape, F32),
                pltpu.VMEM((2, parts, half // parts, depth), F32),
                pltpu.VMEM((2, depth, width), F32),
                pltpu.VMEM((planes, 2, 2, parts, half // parts, depth), F32),
                pltpu.VMEM((2, 3 * depth, 2 * width), BF16),
                pltpu.VMEM((pairs + 3, 2, 2, 2, half, 2 * width), F32),
                pltpu.VMEM((pairs + 3, 2, 2, half, 2 * width), F32),
                pltpu.VMEM((pairs + 3, 2, 2, half, 2 * width), F32),
                pltpu.VMEM((pairs + 3, 2 * groups - 1, 2, rows, 2 * width), F32),
                pltpu.VMEM((pairs + 3, 2, rows, 2 * width), F32),
                pltpu.VMEM((planes, rows, 2 * width), F32),
                pltpu.VMEM((2 * groups, rows, 2 * width), F32),
                dma((2,)),
                dma((planes - 1, 2, 2, parts)),
                dma((planes, 2, 2, parts)),
                dma((2, parts)),
                dma((2, parts)),
                dma((2,)),
                dma((2,)),
                dma((pairs + 4,)),
                dma((pairs + 4,)),
                dma((pairs + 4,)),
                dma((pairs + 4,)),
                dma((1,)),
                dma((1,)),
                dma((1,)),
                dma((1,)),
            ],
            compiler_params=pltpu.CompilerParams(
                collective_id=0, has_side_effects=True, vmem_limit_bytes=54900 << 10
            ),
            cost_estimate=pl.CostEstimate(
                flops=6 * (planes + 1) * 2 * depth * width * 2 * width,
                bytes_accessed=4 * (4 * depth * width + 2 * rows * (planes + 1) * width),
                transcendentals=0,
            ),
        )(psi, h)

    return jax.shard_map(
        shards,
        mesh=mesh,
        in_specs=(P("pw", "band"), P("pw", "band")),
        out_specs=(P(("band", "pw"), None), P(("band", "pw"), None)),
        check_vma=False,
    )
```
